256 devices in a mesh: row: 32 (over x_hi, z, core), col: 8 (over y, x_lo).
Axes of the slice: x: 4 (x_hi: 2, x_lo: 2; x = x_hi * 2 + x_lo), y: 4, z: 8, core: 2. Of those that a mesh axis runs over, the one named last changes fastest.
Arguments:
- out_grad: bfloat16 [1792, 16384], P('row', 'col'), may hold values from -0.8984375 to 0.8984375
- gate_pre: bfloat16 [1792, 28672], P('col', 'row'), may hold values from -9 to 9
- up_pre: bfloat16 [1792, 28672], P('col', 'row'), may hold values from -0.8984375 to 0.8984375
- w_down: bfloat16 [28672, 16384], P('row', 'col'), may hold values from -0.046875 to 0.046875
Outputs:
- grad_down: bfloat16 [28672, 16384], P('row', 'col')
- grad_gate: bfloat16 [1792, 28672], P('col', 'row')
- grad_up: bfloat16 [1792, 28672], P('col', 'row')
The draws below stay inside these ranges and needn't reach their ends.
All inputs are finite; a program needn't handle non-finite values.
Results may differ from the reference program's by a relative error of at most 0.0049.
Values may be sent and summed in bfloat16 or wider, within the bound.
A program may use at most 128 MiB of HBM per device.

```python
import jax
import jax.numpy as jnp

D = 16384
HID = 28672
TOKENS = 1792


def block_scale(own_key, shape, pieces, least, top_value):
    gain = 1.0
    for position, parts in pieces:
        heights = jax.random.uniform(jax.random.fold_in(jax.random.fold_in(own_key, 6), position), (parts,), jnp.float32, least / len(pieces), top_value / len(pieces))
        gain = gain * jnp.repeat(jnp.exp(heights), shape[position] // parts).reshape((-1,) + (1,) * (len(shape) - 1 - position))
    return gain


def bell_draw(stream_key, extent, spread, most, cuts=(), kind=jnp.bfloat16):
    drawn = jax.random.normal(stream_key, extent, jnp.float32) * spread
    if len(cuts) > 0:
        drawn = block_scale(stream_key, extent, cuts, -0.22, 0.18) * drawn
    return jnp.clip(drawn, min=-most, max=most).astype(kind)


def setup_inputs(seed: int = 0) -> dict:
    arg_keys = jax.random.split(jax.random.key(seed), 5)
    return {
        "out_grad": bell_draw(arg_keys[0], (TOKENS, D), 0.15, 0.8984375, ((0, 32), (1, 8))),
        "gate_pre": bell_draw(arg_keys[1], (TOKENS, HID), 1.5, 9.0, ((0, 8), (1, 32))),
        "up_pre": bell_draw(arg_keys[2], (TOKENS, HID), 0.15, 0.8984375, ((0, 8), (1, 32))),
        "w_down": bell_draw(arg_keys[3], (HID, D), D ** -0.5, 0.046875, ((0, 32), (1, 8))),
    }


def reference(out_grad, gate_pre, up_pre, w_down):
    hidden_grad = jnp.dot(out_grad, w_down.T, preferred_element_type=jnp.float32)
    gate = gate_pre.astype(jnp.float32)
    upper = up_pre.astype(jnp.float32)
    sig = jax.nn.sigmoid(gate)
    silu = gate * sig
    hidden = (silu * upper).astype(jnp.bfloat16)
    grad_up = (hidden_grad * silu).astype(jnp.bfloat16)
    grad_gate = (hidden_grad * upper * sig * (1.0 + gate * (1.0 - sig))).astype(jnp.bfloat16)
    grad_down = jnp.dot(hidden.T, out_grad, preferred_element_type=jnp.float32).astype(jnp.bfloat16)
    return grad_down, grad_gate, grad_up
```

```python
import jax
import jax.numpy as jnp
from jax import lax
from jax.experimental import pallas as pl
from jax.experimental.pallas import tpu as pltpu
from jax.sharding import PartitionSpec as P

MESH = pl.DeviceIdType.MESH
BF = jnp.bfloat16
F32 = jnp.float32

TB = 56
UT = 112
H = 896
D = 2048
OT = 224
N1 = 8
N2 = 4
DT = D // N2


def wrap(a, n):
    return lax.rem(a + n, n)


def table(i, values):
    total = jnp.int32(0)
    for k, v in enumerate(values):
        if v != 0:
            total = total + jnp.where(i == k, v, 0)
    return total


MERGED = [0, 1, 1, 3, 3, 5, 5, 7, 8, 8, 8, 8]
SUMMED = [0, 0, 0, 1, 1, 3, 3, 5, 7, 8, 8, 8]
FINISHED = [0, 0, 0, 0, 0, 1, 1, 3, 5, 7, 7, 8]


def kernel(
    og, gate, up, w_hbm, gd_out, gg_out, gu_out,
    panel, w, wt, part, hid, far, near, cross, mine, gate_v, up_v, f_up, f_gate, gg_v, gu_v,
    in_sem, out_sem, gd_sem, ring_recv, sib_recv, up_send, dn_send, sib_send, xh_send,
    hid_recv, half_recv, hy_send, half_send, hx_send,
    far_recv, near_recv, first_send, merge_send, cross_recv, cross_send,
):
    row = lax.axis_index("row")
    col = lax.axis_index("col")
    xh = lax.div(row, 16)
    z = lax.rem(lax.div(row, 2), 8)
    core = lax.rem(row, 2)
    y = lax.div(col, 2)
    xl = lax.rem(col, 2)

    def at(xh_, z_, core_, y_, xl_):
        return ((xh_ * 8 + z_) * 2 + core_, y_ * 2 + xl_)

    z_up = at(xh, wrap(z + 1, 8), core, y, xl)
    z_dn = at(xh, wrap(z - 1, 8), core, y, xl)
    x_far = at(1 - xh, z, core, y, xl)
    sib = at(xh, z, 1 - core, y, xl)
    y_up = at(xh, z, core, wrap(y + 1, 4), xl)
    y_dn = at(xh, z, core, wrap(y - 1, 4), xl)
    x_near = at(xh, z, core, y, 1 - xl)

    def remote(src, dst, ssem, rsem, dev):
        return pltpu.make_async_remote_copy(
            src_ref=src, dst_ref=dst, send_sem=ssem, recv_sem=rsem, device_id=dev, device_id_type=MESH
        )

    load_gate = pltpu.make_async_copy(gate, gate_v, in_sem.at[0])
    load_up = pltpu.make_async_copy(up, up_v, in_sem.at[1])
    load_w = pltpu.make_async_copy(w_hbm, w, in_sem.at[2])
    own_unit = xh * 8 + z
    own_block = own_unit * 2 + core
    load_og = pltpu.make_async_copy(og, panel.at[own_block], in_sem.at[3])

    barrier = pltpu.get_barrier_semaphore()
    for dev in (z_up, z_dn, x_far, sib, y_up, y_dn, x_near):
        pl.semaphore_signal(barrier, inc=1, device_id=dev, device_id_type=MESH)
    load_gate.start()
    load_up.start()
    load_og.start()
    load_w.start()
    pl.semaphore_wait(barrier, 7)

    def ring_copy(unit, ssem, dev, src=None):
        block = panel.at[unit * 2 + core]
        return remote(block if src is None else src, block, ssem.at[unit], ring_recv.at[unit], dev)

    def go_up(unit, src=None):
        return ring_copy(unit, up_send, z_up, src)

    def go_dn(unit, src=None):
        return ring_copy(unit, dn_send, z_dn, src)

    def to_sib(unit, src=None):
        block = panel.at[unit * 2 + core]
        return remote(block if src is None else src, block, sib_send.at[unit], sib_recv.at[unit], sib)

    def from_sib(unit):
        block = panel.at[unit * 2 + 1 - core]
        return remote(block, block, sib_send.at[unit], sib_recv.at[unit], sib)

    def to_far():
        return remote(og, panel.at[own_block], xh_send, ring_recv.at[own_unit], x_far)

    go_up(own_unit, og).start()
    go_dn(own_unit, og).start()
    to_far().start()
    to_sib(own_unit, og).start()

    def hid_copy(c, ssem, dev):
        return remote(hid.at[c], hid.at[c], ssem, hid_recv.at[c], dev)

    def half_copy(c, k, dev):
        block = hid.at[c, pl.ds(UT * k, UT)]
        return remote(block, block, half_send.at[k], half_recv.at[k], dev)

    def hx_copy(y_):
        return hid_copy(y_ * 2 + xl, hx_send.at[y_], x_near)

    y_next, y_prev, y_opp = wrap(y + 1, 4), wrap(y - 1, 4), wrap(y + 2, 4)

    load_gate.wait()
    load_up.wait()

    @pl.loop(0, OT // 16)
    def _(k):
        rows = pl.ds(pl.multiple_of(k * 16, 16), 16)
        g = gate_v[rows, :].astype(F32)
        u = up_v[rows, :].astype(F32)
        s = 1.0 / (1.0 + jnp.exp(-g))
        silu = g * s
        hid[col, rows, :] = (silu * u).astype(BF)
        f_up[rows, :] = silu
        f_gate[rows, :] = u * s * (1.0 + g * (1.0 - s))

    hid_copy(col, hy_send.at[0], y_up).start()
    hid_copy(col, hy_send.at[1], y_dn).start()
    hx_copy(y).start()

    load_w.wait()

    @pl.loop(0, 8)
    def _(k):
        cols = pl.ds(pl.multiple_of(k * 256, 256), 256)
        wt[cols, :] = w[:, cols].T

    far_unit = (1 - xh) * 8 + z
    ring_copy(far_unit, up_send, z_up).wait_recv()
    go_up(far_unit).start()
    go_dn(far_unit).start()
    to_sib(far_unit).start()
    load_og.wait()

    def pass_on(d, xh_):
        from_dn = xh_ * 8 + wrap(z - d, 8)
        go_up(from_dn).wait_recv()

        @pl.when(jnp.logical_or(d < 3, xh_ == 0))
        def _():
            go_up(from_dn).start()

        to_sib(from_dn).start()
        from_up = xh_ * 8 + wrap(z + d, 8)
        go_dn(from_up).wait_recv()

        @pl.when(jnp.logical_or(d < 3, xh_ == 1))
        def _():
            go_dn(from_up).start()

        to_sib(from_up).start()

    def z_of(q):
        return wrap(z + lax.div(q + 1, 2) * (1 - 2 * lax.rem(q, 2)), 8)

    y_half = lax.div(y, 2)

    def at_end(zq):
        return lax.div(zq, 4) == lax.rem(y, 2)

    def far_copy(zq, dev):
        unit = (1 - y_half) * 8 + zq
        return remote(part.at[unit], far.at[lax.rem(zq, 4)], first_send.at[zq], far_recv.at[lax.rem(zq, 4)], dev)

    def near_copy(y_to, side, zq, sem, dev):
        unit = lax.div(y_to, 2) * 8 + zq
        k = lax.rem(zq, 4)
        return remote(part.at[unit], near.at[side, k], sem, near_recv.at[side, k], dev)

    def first_sends(zq):
        even = lax.rem(zq, 2) == 0
        end = at_end(zq)

        @pl.when(jnp.logical_and(end, even))
        def _():
            far_copy(zq, y_dn).start()

        @pl.when(jnp.logical_and(end, jnp.logical_not(even)))
        def _():
            far_copy(zq, y_up).start()

        @pl.when(jnp.logical_and(jnp.logical_not(end), even))
        def _():
            near_copy(y_next, 0, zq, first_send.at[zq], y_up).start()

        @pl.when(jnp.logical_and(jnp.logical_not(end), jnp.logical_not(even)))
        def _():
            near_copy(y_prev, 1, zq, first_send.at[zq], y_dn).start()

    def merge(zq):
        @pl.when(jnp.logical_not(at_end(zq)))
        def _():
            k = lax.rem(zq, 4)
            even = lax.rem(zq, 2) == 0
            y_to = jnp.where(even, y_prev, y_next)
            unit = lax.div(y_to, 2) * 8 + zq
            far_copy(zq, y_up).wait_recv()

            @pl.loop(0, UT // 16)
            def _(r):
                rows = pl.ds(pl.multiple_of(r * 16, 16), 16)
                part[unit, rows, :] = (part[unit, rows, :].astype(F32) + far[k, rows, :].astype(F32)).astype(BF)

            @pl.when(even)
            def _():
                near_copy(y_prev, 1, zq, merge_send.at[k], y_dn).start()

            @pl.when(jnp.logical_not(even))
            def _():
                near_copy(y_next, 0, zq, merge_send.at[k], y_up).start()

    def is_mine(zq):
        return lax.rem(lax.div(zq, 2), 2) == xl

    def cross_copy(zq):
        k = lax.rem(zq, 2)
        return remote(part.at[y_half * 8 + zq], cross.at[k], cross_send.at[k], cross_recv.at[k], x_near)

    def sum_up(zq):
        @pl.when(at_end(zq))
        def _():
            k = lax.rem(zq, 4)
            unit = y_half * 8 + zq
            near_copy(y, 0, zq, first_send.at[zq], y_dn).wait_recv()
            near_copy(y, 1, zq, first_send.at[zq], y_up).wait_recv()
            own = is_mine(zq)

            def total(rows):
                return part[unit, rows, :].astype(F32) + (
                    near[0, k, rows, :].astype(F32) + near[1, k, rows, :].astype(F32)
                )

            @pl.when(own)
            def _():
                @pl.loop(0, UT // 16)
                def _(r):
                    rows = pl.ds(pl.multiple_of(r * 16, 16), 16)
                    mine[lax.rem(zq, 2), rows, :] = total(rows)

            @pl.when(jnp.logical_not(own))
            def _():
                @pl.loop(0, UT // 16)
                def _(r):
                    rows = pl.ds(pl.multiple_of(r * 16, 16), 16)
                    part[unit, rows, :] = total(rows).astype(BF)

                cross_copy(zq).start()

    def out_copies(k):
        rows = pl.ds(pl.multiple_of(k * UT, 16), UT)
        return (
            pltpu.make_async_copy(gg_v.at[rows], gg_out.at[rows], out_sem.at[0, k]),
            pltpu.make_async_copy(gu_v.at[rows], gu_out.at[rows], out_sem.at[1, k]),
        )

    def finish(zq):
        @pl.when(jnp.logical_and(at_end(zq), is_mine(zq)))
        def _():
            k = lax.rem(zq, 2)
            cross_copy(zq).wait_recv()

            @pl.loop(0, UT // 16)
            def _(r):
                rows = pl.ds(pl.multiple_of(r * 16, 16), 16)
                here = pl.ds(pl.multiple_of(k * UT + r * 16, 16), 16)
                grad = mine[k, rows, :] + cross[k, rows, :].astype(F32)
                gu_v[here, :] = (grad * f_up[here, :]).astype(BF)
                gg_v[here, :] = (grad * f_gate[here, :]).astype(BF)

            for c in out_copies(k):
                c.start()

    def gd_copy(t):
        cols = pl.ds(pl.multiple_of(t * DT, DT), DT)
        return pltpu.make_async_copy(w.at[:, cols], gd_out.at[:, cols], gd_sem.at[t])

    @pl.loop(0, N1 + N2)
    def _(i):
        odd = lax.rem(i, 2) == 1

        @pl.when(jnp.logical_and(odd, i < 7))
        def _():
            d = lax.div(i + 1, 2)
            pass_on(d, xh)
            pass_on(d, 1 - xh)

        z_opp = wrap(z + 4, 8)

        @pl.when(i == 7)
        def _():
            go_up(z_opp).wait_recv()
            to_sib(z_opp).start()
            go_dn(8 + z_opp).wait_recv()
            to_sib(8 + z_opp).start()

        @pl.when(i < N1)
        def _():
            zq = z_of(i)
            from_sib(zq).wait_recv()
            from_sib(8 + zq).wait_recv()
            lhs = jnp.concatenate(
                [panel[pl.ds(2 * zq, 2)].reshape(UT, D), panel[pl.ds(16 + 2 * zq, 2)].reshape(UT, D)], axis=0
            )
            res = lax.dot_general(lhs, wt[...], (((1,), (0,)), ((), ())), preferred_element_type=F32).astype(BF)
            part[zq] = res[:UT]
            part[8 + zq] = res[UT:]
            first_sends(zq)

        @pl.when(i == 1)
        def _():
            hid_copy(y_next * 2 + xl, hy_send.at[0], y_up).wait_recv()
            half_copy(y_next * 2 + xl, 0, y_dn).start()
            hx_copy(y_next).start()
            hid_copy(y_prev * 2 + xl, hy_send.at[1], y_dn).wait_recv()
            half_copy(y_prev * 2 + xl, 1, y_up).start()
            hx_copy(y_prev).start()

        @pl.when(i == 3)
        def _():
            half_copy(y_opp * 2 + xl, 0, y_up).wait_recv()
            half_copy(y_opp * 2 + xl, 1, y_dn).wait_recv()
            hx_copy(y_opp).start()

        @pl.when(i == N1)
        def _():
            for y_ in range(4):
                hid_copy(y_ * 2 + 1 - xl, hx_send.at[y_], x_near).wait_recv()

        @pl.when(i >= N1)
        def _():
            t = i - N1
            cols = pl.ds(pl.multiple_of(t * DT, DT), DT)
            res = lax.dot_general(
                hid[...].reshape(8 * OT, H),
                panel[:, :, cols].reshape(8 * OT, DT),
                (((0,), (0,)), ((), ())),
                preferred_element_type=F32,
            )
            w[:, cols] = res.astype(BF)
            gd_copy(t).start()

        before = jnp.maximum(i - 1, 0)

        @pl.loop(table(before, MERGED), table(i, MERGED))
        def _(q):
            merge(z_of(q))

        @pl.loop(table(before, SUMMED), table(i, SUMMED))
        def _(q):
            sum_up(z_of(q))

        @pl.loop(table(before, FINISHED), table(i, FINISHED))
        def _(q):
            finish(z_of(q))

    to_far().wait_send()

    @pl.loop(0, 4)
    def _(d):
        for xh_ in range(2):
            below = xh_ * 8 + wrap(z - d, 8)
            above = xh_ * 8 + wrap(z + d, 8)

            @pl.when(jnp.logical_or(d < 3, xh_ == 0))
            def _():
                go_up(below).wait_send()

            @pl.when(jnp.logical_or(d < 3, xh_ == 1))
            def _():
                go_dn(above).wait_send()

    @pl.loop(0, 16)
    def _(u):
        to_sib(u).wait_send()

    hid_copy(col, hy_send.at[0], y_up).wait_send()
    hid_copy(col, hy_send.at[1], y_dn).wait_send()
    half_copy(col, 0, y_dn).wait_send()
    half_copy(col, 1, y_up).wait_send()
    for y_ in range(4):
        hx_copy(y_).wait_send()

    @pl.loop(0, 8)
    def _(zq):
        far_copy(zq, y_up).wait_send()

        @pl.when(jnp.logical_not(at_end(zq)))
        def _():
            near_copy(y_next, 0, zq, merge_send.at[lax.rem(zq, 4)], y_up).wait_send()

    for k in range(2):
        cross_copy(k).wait_send()
        for c in out_copies(k):
            c.wait()
    for t in range(N2):
        gd_copy(t).wait()


def on_device(out_grad, gate_pre, up_pre, w_down):
    dma = pltpu.SemaphoreType.DMA
    any_space = pl.BlockSpec(memory_space=pl.ANY)
    return pl.pallas_call(
        kernel,
        out_shape=(
            jax.ShapeDtypeStruct((H, D), BF),
            jax.ShapeDtypeStruct((OT, H), BF),
            jax.ShapeDtypeStruct((OT, H), BF),
        ),
        in_specs=[any_space] * 4,
        out_specs=(any_space,) * 3,
        scratch_shapes=[
            pltpu.VMEM((32, TB, D), BF),
            pltpu.VMEM((H, D), BF),
            pltpu.VMEM((D, H), BF),
            pltpu.VMEM((16, UT, H), BF),
            pltpu.VMEM((8, OT, H), BF),
            pltpu.VMEM((4, UT, H), BF),
            pltpu.VMEM((2, 4, UT, H), BF),
            pltpu.VMEM((2, UT, H), BF),
            pltpu.VMEM((2, UT, H), F32),
            pltpu.VMEM((OT, H), BF),
            pltpu.VMEM((OT, H), BF),
            pltpu.VMEM((OT, H), F32),
            pltpu.VMEM((OT, H), F32),
            pltpu.VMEM((OT, H), BF),
            pltpu.VMEM((OT, H), BF),
            dma((4,)), dma((2, 2)), dma((N2,)),
            dma((16,)), dma((16,)), dma((16,)), dma((16,)), dma((16,)), dma,
            dma((8,)), dma((2,)), dma((2,)), dma((2,)), dma((4,)),
            dma((4,)), dma((2, 4)), dma((8,)), dma((4,)), dma((2,)), dma((2,)),
        ],
        compiler_params=pltpu.CompilerParams(
            collective_id=0, has_side_effects=True, vmem_limit_bytes=56 * 2**20
        ),
        cost_estimate=pl.CostEstimate(flops=4 * 1792 * H * D, bytes_accessed=9 * 2**20, transcendentals=OT * H),
        name="swiglu_down_backward",
    )(out_grad, gate_pre, up_pre, w_down)


def solution(mesh):
    return jax.shard_map(
        on_device,
        mesh=mesh,
        in_specs=(P("row", "col"), P("col", "row"), P("col", "row"), P("row", "col")),
        out_specs=(P("row", "col"), P("col", "row"), P("col", "row")),
        check_vma=False,
    )
```

```python
import jax
import jax.numpy as jnp
from jax import lax
from jax.experimental import pallas as pl
from jax.experimental.pallas import tpu as pltpu
from jax.sharding import PartitionSpec as P

MESH = pl.DeviceIdType.MESH
BF = jnp.bfloat16
F32 = jnp.float32

TB = 56
UT = 112
HALVES = ((0, 64), (64, 48))
H = 896
D = 2048
DH = D // 2
OT = 224
N1 = 9
N2 = 4
DT = D // N2


def wrap(a, n):
    return lax.rem(a + n, n)


def table(i, values):
    total = jnp.int32(0)
    for k, v in enumerate(values):
        if v != 0:
            total = total + jnp.where(i == k, v, 0)
    return total


MERGED = [0, 0, 2, 3, 5, 7, 9, 9, 14, 16, 16, 16, 16]
SUMMED = [0, 0, 0, 0, 2, 3, 5, 5, 9, 14, 16, 16, 16]
FINISHED = [0, 0, 0, 0, 0, 0, 2, 2, 5, 9, 14, 14, 16]
HID_NEAR = 2
HID_FAR = 4


def kernel(
    og, gate, up, w_hbm, gd_out, gg_out, gu_out,
    panel, w, wt, part, hid, far, near, cross, mine, gate_v, up_v, f_up, f_gate,
    in_sem, ring_recv, sib_recv, up_send, dn_send, sib_send, xh_send,
    hid_recv, hup_send, hdn_send, hx_send,
    far_recv, near_recv, first_send, merge_send, cross_recv, cross_send,
):
    row = lax.axis_index("row")
    col = lax.axis_index("col")
    xh = lax.div(row, 16)
    z = lax.rem(lax.div(row, 2), 8)
    core = lax.rem(row, 2)
    y = lax.div(col, 2)
    xl = lax.rem(col, 2)

    def at(xh_, z_, core_, y_, xl_):
        return ((xh_ * 8 + z_) * 2 + core_, y_ * 2 + xl_)

    y_next, y_prev, y_opp = wrap(y + 1, 4), wrap(y - 1, 4), wrap(y + 2, 4)
    z_up = at(xh, wrap(z + 1, 8), core, y, xl)
    z_dn = at(xh, wrap(z - 1, 8), core, y, xl)
    x_far = at(1 - xh, z, core, y, xl)
    sib = at(xh, z, 1 - core, y, xl)
    y_up = at(xh, z, core, y_next, xl)
    y_dn = at(xh, z, core, y_prev, xl)
    x_near = at(xh, z, core, y, 1 - xl)

    def remote(src, dst, ssem, rsem, dev):
        return pltpu.make_async_remote_copy(
            src_ref=src, dst_ref=dst, send_sem=ssem, recv_sem=rsem, device_id=dev, device_id_type=MESH
        )

    load_gate = pltpu.make_async_copy(gate, gate_v, in_sem.at[0])
    load_up = pltpu.make_async_copy(up, up_v, in_sem.at[1])
    load_w = pltpu.make_async_copy(w_hbm, w, in_sem.at[2])
    own_unit = xh * 8 + z
    far_unit = (1 - xh) * 8 + z
    load_og = pltpu.make_async_copy(og, panel.at[own_unit * 2 + core], in_sem.at[3])

    barrier = pltpu.get_barrier_semaphore()
    for dev in (z_up, z_dn, x_far, sib, y_up, y_dn, x_near):
        pl.semaphore_signal(barrier, inc=1, device_id=dev, device_id_type=MESH)
    load_gate.start()
    load_up.start()
    load_og.start()
    load_w.start()
    pl.semaphore_wait(barrier, 7)

    def half(j):
        return pl.ds(j * DH, DH)

    def ring_copy(unit, j, ssem, dev, own=False):
        block = panel.at[unit * 2 + core, :, half(j)]
        return remote(og.at[:, half(j)] if own else block, block, ssem, ring_recv.at[j, unit], dev)

    def go_up(unit, j, own=False):
        return ring_copy(unit, j, up_send.at[j, unit], z_up, own)

    def go_dn(unit, j, own=False):
        return ring_copy(unit, j, dn_send.at[j, unit], z_dn, own)

    def to_far(j):
        return ring_copy(own_unit, j, xh_send.at[j], x_far, True)

    def sib_copy(unit, j, core_, own=False):
        block = panel.at[unit * 2 + core_, :, half(j)]
        return remote(
            og.at[:, half(j)] if own else block, block, sib_send.at[j, unit], sib_recv.at[j, unit], sib
        )

    def to_sib(unit, j, own=False):
        return sib_copy(unit, j, core, own)

    for j in range(2):
        to_far(j).start()
        go_up(own_unit, j, True).start()
        go_dn(own_unit, j, True).start()
    for j in range(2):
        to_sib(own_unit, j, True).start()

    def hid_copy(c, ssem, dev):
        return remote(hid.at[c], hid.at[c], ssem, hid_recv.at[c], dev)

    load_gate.wait()
    load_up.wait()

    @pl.loop(0, OT // 16)
    def _(k):
        rows = pl.ds(pl.multiple_of(k * 16, 16), 16)
        g = gate_v[rows, :].astype(F32)
        u = up_v[rows, :].astype(F32)
        s = 1.0 / (1.0 + jnp.exp(-g))
        silu = g * s
        hid[col, rows, :] = (silu * u).astype(BF)
        f_up[rows, :] = silu
        f_gate[rows, :] = u * s * (1.0 + g * (1.0 - s))

    c_next, c_prev, c_opp = y_next * 2 + xl, y_prev * 2 + xl, y_opp * 2 + xl
    p_own, p_next, p_prev, p_opp = (y_ * 2 + 1 - xl for y_ in (y, y_next, y_prev, y_opp))
    hid_copy(col, hup_send.at[0], y_up).start()
    hid_copy(col, hdn_send.at[0], y_dn).start()
    hid_copy(col, hx_send.at[0], x_near).start()

    def pass_on(d, xh_):
        from_dn = xh_ * 8 + wrap(z - d, 8)
        from_up = xh_ * 8 + wrap(z + d, 8)
        for j in range(2):
            go_up(from_dn, j).wait_recv()

            @pl.when(jnp.logical_or(d < 3, xh_ == 0))
            def _():
                go_up(from_dn, j).start()

            to_sib(from_dn, j).start()
            go_dn(from_up, j).wait_recv()

            @pl.when(jnp.logical_or(d < 3, xh_ == 1))
            def _():
                go_dn(from_up, j).start()

            to_sib(from_up, j).start()

    for j in range(2):
        to_far_in = ring_copy(far_unit, j, xh_send.at[j], x_far)
        to_far_in.wait_recv()
        go_up(far_unit, j).start()
        go_dn(far_unit, j).start()
        to_sib(far_unit, j).start()
    pass_on(1, xh)

    load_w.wait()

    @pl.loop(0, 8)
    def _(k):
        cols = pl.ds(pl.multiple_of(k * 256, 256), 256)
        wt[cols, :] = w[:, cols].T

    load_og.wait()

    def unit(k):
        d = lax.div(k + 2, 4)
        own = jnp.logical_or(k == 0, jnp.logical_and(lax.rem(k + 2, 4) < 2, k < 15))
        return jnp.where(own, xh, 1 - xh) * 8 + jnp.where(lax.rem(k, 2) == 0, wrap(z - d, 8), wrap(z + d, 8))

    def distance(m):
        return wrap(y - lax.div(m, 4), 4)

    def rows_of(hf):
        return pl.ds(HALVES[hf][0], HALVES[hf][1])

    def far_copy(m, hf, dev):
        k = hf * 4 + lax.rem(m, 4)
        return remote(
            part.at[m, rows_of(hf)], far.at[k, pl.ds(0, HALVES[hf][1])], first_send.at[hf, m], far_recv.at[k], dev
        )

    def near_copy(m, hf, side, sem, dev):
        k = lax.rem(m, 4)
        return remote(
            part.at[m, rows_of(hf)], near.at[side, k, rows_of(hf)], sem, near_recv.at[side, k, hf], dev
        )

    def first_sends(m):
        d = distance(m)

        @pl.when(d == 2)
        def _():
            far_copy(m, 0, y_dn).start()
            far_copy(m, 1, y_up).start()

        @pl.when(d == 1)
        def _():
            near_copy(m, 1, 1, first_send.at[1, m], y_dn).start()

        @pl.when(d == 3)
        def _():
            near_copy(m, 0, 0, first_send.at[0, m], y_up).start()

    def row_loop(hf):
        return pl.loop(0, HALVES[hf][1] // 16)

    def merge(m):
        d = distance(m)
        for hf in range(2):

            @pl.when(d == 1 + 2 * hf)
            def _():
                far_copy(m, hf, y_up if hf == 0 else y_dn).wait_recv()
                k = hf * 4 + lax.rem(m, 4)

                @row_loop(hf)
                def _(r):
                    rows = pl.ds(pl.multiple_of(HALVES[hf][0] + r * 16, 16), 16)
                    theirs = far[k, pl.ds(pl.multiple_of(r * 16, 16), 16), :]
                    part[m, rows, :] = (part[m, rows, :].astype(F32) + theirs.astype(F32)).astype(BF)

                near_copy(m, hf, 1 - hf, merge_send.at[m], y_dn if hf == 0 else y_up).start()

    def is_mine(m):
        return lax.rem(lax.div(m, 2), 2) == xl

    def cross_copy(m, hf):
        k = lax.rem(m, 2)
        return remote(
            part.at[m, rows_of(hf)], cross.at[k, rows_of(hf)], cross_send.at[k, hf], cross_recv.at[k, hf], x_near
        )

    def sum_up(m):
        @pl.when(distance(m) == 0)
        def _():
            k = lax.rem(m, 4)
            own = is_mine(m)
            for hf in range(2):
                near_copy(m, hf, 0, first_send.at[hf, m], y_dn).wait_recv()
                near_copy(m, hf, 1, first_send.at[hf, m], y_up).wait_recv()

                def total(r):
                    rows = pl.ds(pl.multiple_of(HALVES[hf][0] + r * 16, 16), 16)
                    sides = near[0, k, rows, :].astype(F32) + near[1, k, rows, :].astype(F32)
                    return rows, part[m, rows, :].astype(F32) + sides

                @pl.when(own)
                def _():
                    @row_loop(hf)
                    def _(r):
                        rows, value = total(r)
                        mine[lax.rem(m, 2), rows, :] = value

                @pl.when(jnp.logical_not(own))
                def _():
                    @row_loop(hf)
                    def _(r):
                        rows, value = total(r)
                        part[m, rows, :] = value.astype(BF)

                    cross_copy(m, hf).start()

    def finish(m):
        @pl.when(jnp.logical_and(distance(m) == 0, is_mine(m)))
        def _():
            k = lax.rem(m, 2)
            for hf in range(2):
                cross_copy(m, hf).wait_recv()

                @row_loop(hf)
                def _(r):
                    rows = pl.ds(pl.multiple_of(HALVES[hf][0] + r * 16, 16), 16)
                    here = pl.ds(pl.multiple_of(k * UT + HALVES[hf][0] + r * 16, 16), 16)
                    grad = mine[k, rows, :] + cross[k, rows, :].astype(F32)
                    gu_out[here, :] = (grad * f_up[here, :]).astype(BF)
                    gg_out[here, :] = (grad * f_gate[here, :]).astype(BF)

    @pl.loop(0, N1 + N2)
    def _(i):
        @pl.when(i < N1)
        def _():
            k0 = 2 * i - 1 + jnp.where(i < 2, 1, 0) - jnp.where(i == 8, 1, 0)
            both = jnp.logical_and(i != 1, i != 7)
            m0 = unit(k0)
            m1 = jnp.where(both, unit(k0 + 1), m0)
            for j in range(2):
                sib_copy(m0, j, 1 - core).wait_recv()

            @pl.when(both)
            def _():
                for j in range(2):
                    sib_copy(m1, j, 1 - core).wait_recv()

            lhs = jnp.concatenate(
                [panel[pl.ds(2 * m0, 2)].reshape(UT, D), panel[pl.ds(2 * m1, 2)].reshape(UT, D)], axis=0
            )
            res = lax.dot_general(lhs, wt[...], (((1,), (0,)), ((), ())), preferred_element_type=F32).astype(BF)
            part[m0] = res[:UT]
            first_sends(m0)

            @pl.when(both)
            def _():
                part[m1] = res[UT:]
                first_sends(m1)

        @pl.when(i == N1)
        def _():
            hid_copy(c_opp, hup_send.at[1], y_dn).wait_recv()
            hid_copy(p_own, hx_send.at[0], x_near).wait_recv()
            hid_copy(p_prev, hx_send.at[2], x_near).wait_recv()
            hid_copy(p_opp, hdn_send.at[1], y_up).wait_recv()

        @pl.when(i >= N1)
        def _():
            t = i - N1
            cols = pl.ds(pl.multiple_of(t * DT, DT), DT)
            res = lax.dot_general(
                hid[...].reshape(8 * OT, H),
                panel[:, :, cols].reshape(8 * OT, DT),
                (((0,), (0,)), ((), ())),
                preferred_element_type=F32,
            )
            gd_out[:, cols] = res.astype(BF)

        before = jnp.maximum(i - 1, 0)

        @pl.loop(table(before, MERGED), table(i, MERGED))
        def _(k):
            merge(unit(k))

        @pl.loop(table(before, SUMMED), table(i, SUMMED))
        def _(k):
            sum_up(unit(k))

        @pl.loop(table(before, FINISHED), table(i, FINISHED))
        def _(k):
            finish(unit(k))

        @pl.when(i == HID_NEAR)
        def _():
            hid_copy(c_next, hup_send.at[0], y_up).wait_recv()
            hid_copy(c_next, hx_send.at[1], x_near).start()
            hid_copy(c_prev, hdn_send.at[0], y_dn).wait_recv()
            hid_copy(c_prev, hup_send.at[1], y_up).start()
            hid_copy(c_prev, hx_send.at[2], x_near).start()

        @pl.when(i == HID_FAR)
        def _():
            hid_copy(p_next, hx_send.at[1], x_near).wait_recv()
            hid_copy(p_next, hdn_send.at[1], y_dn).start()

        @pl.when(jnp.logical_and(i >= 1, i < 6))
        def _():
            pass_on(lax.div(i + 2, 2), jnp.where(lax.rem(i, 2) == 0, xh, 1 - xh))

        @pl.when(i == 7)
        def _():
            z_opp = wrap(z + 4, 8)
            for j in range(2):
                go_up(z_opp, j).wait_recv()
                to_sib(z_opp, j).start()
                go_dn(8 + z_opp, j).wait_recv()
                to_sib(8 + z_opp, j).start()

    for j in range(2):
        to_far(j).wait_send()

    @pl.loop(0, 4)
    def _(d):
        for xh_ in range(2):
            below = xh_ * 8 + wrap(z - d, 8)
            above = xh_ * 8 + wrap(z + d, 8)

            @pl.when(jnp.logical_or(d < 3, xh_ == 0))
            def _():
                for j in range(2):
                    go_up(below, j).wait_send()

            @pl.when(jnp.logical_or(d < 3, xh_ == 1))
            def _():
                for j in range(2):
                    go_dn(above, j).wait_send()

    @pl.loop(0, 16)
    def _(m):
        for j in range(2):
            to_sib(m, j).wait_send()
        d = distance(m)

        @pl.when(d >= 2)
        def _():
            far_copy(m, 0, y_dn).wait_send()

        @pl.when(jnp.logical_or(d == 1, d == 2))
        def _():
            far_copy(m, 1, y_up).wait_send()

        for hf in range(2):

            @pl.when(d == 1 + 2 * hf)
            def _():
                near_copy(m, hf, 1 - hf, merge_send.at[m], y_dn if hf == 0 else y_up).wait_send()

    for k in range(2):
        hid_copy(col, hup_send.at[k], y_up).wait_send()
        hid_copy(col, hdn_send.at[k], y_dn).wait_send()
    for k in range(3):
        hid_copy(col, hx_send.at[k], x_near).wait_send()
    for k in range(2):
        for hf in range(2):
            cross_copy(k, hf).wait_send()


def on_device(out_grad, gate_pre, up_pre, w_down):
    dma = pltpu.SemaphoreType.DMA
    any_space = pl.BlockSpec(memory_space=pl.ANY)
    return pl.pallas_call(
        kernel,
        out_shape=(
            pltpu.VMEM((H, D), BF),
            pltpu.VMEM((OT, H), BF),
            pltpu.VMEM((OT, H), BF),
        ),
        in_specs=[any_space] * 4,
        out_specs=(pl.BlockSpec(memory_space=pltpu.VMEM),) * 3,
        scratch_shapes=[
            pltpu.VMEM((32, TB, D), BF),
            pltpu.VMEM((H, D), BF),
            pltpu.VMEM((D, H), BF),
            pltpu.VMEM((16, UT, H), BF),
            pltpu.VMEM((8, OT, H), BF),
            pltpu.VMEM((8, HALVES[0][1], H), BF),
            pltpu.VMEM((2, 4, UT, H), BF),
            pltpu.VMEM((2, UT, H), BF),
            pltpu.VMEM((2, UT, H), F32),
            pltpu.VMEM((OT, H), BF),
            pltpu.VMEM((OT, H), BF),
            pltpu.VMEM((OT, H), F32),
            pltpu.VMEM((OT, H), F32),
            dma((4,)),
            dma((2, 16)), dma((2, 16)), dma((2, 16)), dma((2, 16)), dma((2, 16)), dma((2,)),
            dma((8,)), dma((2,)), dma((2,)), dma((3,)),
            dma((8,)), dma((2, 4, 2)), dma((2, 16)), dma((16,)), dma((2, 2)), dma((2, 2)),
        ],
        compiler_params=pltpu.CompilerParams(
            collective_id=0, has_side_effects=True, vmem_limit_bytes=56 * 2**20
        ),
        cost_estimate=pl.CostEstimate(flops=4 * 1792 * H * D, bytes_accessed=9 * 2**20, transcendentals=OT * H),
        name="swiglu_down_backward",
    )(out_grad, gate_pre, up_pre, w_down)


def solution(mesh):
    return jax.shard_map(
        on_device,
        mesh=mesh,
        in_specs=(P("row", "col"), P("col", "row"), P("col", "row"), P("row", "col")),
        out_specs=(P("row", "col"), P("col", "row"), P("col", "row")),
        check_vma=False,
    )
```

```python
import jax
import jax.numpy as jnp
from jax import lax
from jax.experimental import pallas as pl
from jax.experimental.pallas import tpu as pltpu
from jax.sharding import PartitionSpec as P

MESH = pl.DeviceIdType.MESH
BF = jnp.bfloat16
F32 = jnp.float32

TB = 56
UT = 112
HALVES = ((0, 64), (64, 48))
H = 896
D = 2048
DH = D // 2
OT = 224
N1 = 9
N2 = 4
DT = D // N2


def wrap(a, n):
    return lax.rem(a + n, n)


def table(i, values):
    total = jnp.int32(0)
    for k, v in enumerate(values):
        if v != 0:
            total = total + jnp.where(i == k, v, 0)
    return total


MERGED = [0, 0, 2, 3, 5, 7, 9, 11, 11, 14, 16, 16, 16, 16]
SUMMED = [0, 0, 0, 0, 2, 3, 5, 7, 7, 11, 14, 16, 16, 16]
FINISHED = [0, 0, 0, 0, 0, 0, 2, 3, 3, 7, 11, 14, 14, 16]
HID_NEAR = 2
HID_FAR = 4


def kernel(
    og, gate, up, w_hbm, gd_out, gg_out, gu_out,
    panel, w, wt, part, hid, far, near, cross, mine, gate_v, up_v, f_up, f_gate,
    in_sem, ring_recv, sib_recv, up_send, dn_send, sib_send, xh_send,
    hid_recv, hup_send, hdn_send, hx_send,
    far_recv, near_recv, first_send, merge_send, cross_recv, cross_send,
):
    row = lax.axis_index("row")
    col = lax.axis_index("col")
    xh = lax.div(row, 16)
    z = lax.rem(lax.div(row, 2), 8)
    core = lax.rem(row, 2)
    y = lax.div(col, 2)
    xl = lax.rem(col, 2)

    def at(xh_, z_, core_, y_, xl_):
        return ((xh_ * 8 + z_) * 2 + core_, y_ * 2 + xl_)

    y_next, y_prev, y_opp = wrap(y + 1, 4), wrap(y - 1, 4), wrap(y + 2, 4)
    z_up = at(xh, wrap(z + 1, 8), core, y, xl)
    z_dn = at(xh, wrap(z - 1, 8), core, y, xl)
    x_far = at(1 - xh, z, core, y, xl)
    sib = at(xh, z, 1 - core, y, xl)
    y_up = at(xh, z, core, y_next, xl)
    y_dn = at(xh, z, core, y_prev, xl)
    x_near = at(xh, z, core, y, 1 - xl)

    def remote(src, dst, ssem, rsem, dev):
        return pltpu.make_async_remote_copy(
            src_ref=src, dst_ref=dst, send_sem=ssem, recv_sem=rsem, device_id=dev, device_id_type=MESH
        )

    load_gate = pltpu.make_async_copy(gate, gate_v, in_sem.at[0])
    load_up = pltpu.make_async_copy(up, up_v, in_sem.at[1])
    load_w = pltpu.make_async_copy(w_hbm, w, in_sem.at[2])
    own_unit = xh * 8 + z
    far_unit = (1 - xh) * 8 + z
    load_og = pltpu.make_async_copy(og, panel.at[own_unit * 2 + core], in_sem.at[3])

    barrier = pltpu.get_barrier_semaphore()
    for dev in (z_up, z_dn, x_far, sib, y_up, y_dn, x_near):
        pl.semaphore_signal(barrier, inc=1, device_id=dev, device_id_type=MESH)
    load_gate.start()
    load_up.start()
    load_og.start()
    load_w.start()
    pl.semaphore_wait(barrier, 7)

    def half(j):
        return pl.ds(j * DH, DH)

    def ring_copy(unit, j, ssem, dev, own=False):
        block = panel.at[unit * 2 + core, :, half(j)]
        return remote(og.at[:, half(j)] if own else block, block, ssem, ring_recv.at[j, unit], dev)

    def go_up(unit, j, own=False):
        return ring_copy(unit, j, up_send.at[j, unit], z_up, own)

    def go_dn(unit, j, own=False):
        return ring_copy(unit, j, dn_send.at[j, unit], z_dn, own)

    def to_far(j):
        return ring_copy(own_unit, j, xh_send.at[j], x_far, True)

    def sib_copy(unit, j, core_, own=False):
        block = panel.at[unit * 2 + core_, :, half(j)]
        return remote(
            og.at[:, half(j)] if own else block, block, sib_send.at[j, unit], sib_recv.at[j, unit], sib
        )

    def to_sib(unit, j, own=False):
        return sib_copy(unit, j, core, own)

    for j in range(2):
        to_far(j).start()
        go_up(own_unit, j, True).start()
        go_dn(own_unit, j, True).start()
    for j in range(2):
        to_sib(own_unit, j, True).start()

    def hid_copy(c, ssem, dev):
        return remote(hid.at[c], hid.at[c], ssem, hid_recv.at[c], dev)

    load_gate.wait()
    load_up.wait()

    @pl.loop(0, OT // 16)
    def _(k):
        rows = pl.ds(pl.multiple_of(k * 16, 16), 16)
        g = gate_v[rows, :].astype(F32)
        u = up_v[rows, :].astype(F32)
        s = 1.0 / (1.0 + jnp.exp(-g))
        silu = g * s
        hid[col, rows, :] = (silu * u).astype(BF)
        f_up[rows, :] = silu
        f_gate[rows, :] = u * s * (1.0 + g * (1.0 - s))

    c_next, c_prev, c_opp = y_next * 2 + xl, y_prev * 2 + xl, y_opp * 2 + xl
    p_own, p_next, p_prev, p_opp = (y_ * 2 + 1 - xl for y_ in (y, y_next, y_prev, y_opp))
    hid_copy(col, hup_send.at[0], y_up).start()
    hid_copy(col, hdn_send.at[0], y_dn).start()

    def pass_on(d, xh_):
        from_dn = xh_ * 8 + wrap(z - d, 8)
        from_up = xh_ * 8 + wrap(z + d, 8)
        for j in range(2):
            go_up(from_dn, j).wait_recv()

            @pl.when(jnp.logical_or(d < 3, xh_ == 0))
            def _():
                go_up(from_dn, j).start()

            to_sib(from_dn, j).start()
            go_dn(from_up, j).wait_recv()

            @pl.when(jnp.logical_or(d < 3, xh_ == 1))
            def _():
                go_dn(from_up, j).start()

            to_sib(from_up, j).start()

    load_w.wait()

    @pl.loop(0, 8)
    def _(k):
        cols = pl.ds(pl.multiple_of(k * 256, 256), 256)
        wt[cols, :] = w[:, cols].T

    for j in range(2):
        to_far_in = ring_copy(far_unit, j, xh_send.at[j], x_far)
        to_far_in.wait_recv()
        go_up(far_unit, j).start()
        go_dn(far_unit, j).start()
        to_sib(far_unit, j).start()
    hid_copy(col, hx_send.at[0], x_near).start()
    pass_on(1, xh)

    load_og.wait()

    def unit(k):
        d = lax.div(k + 2, 4)
        own = jnp.logical_or(k == 0, jnp.logical_and(lax.rem(k + 2, 4) < 2, k < 15))
        return jnp.where(own, xh, 1 - xh) * 8 + jnp.where(lax.rem(k, 2) == 0, wrap(z - d, 8), wrap(z + d, 8))

    def distance(m):
        return wrap(y - lax.div(m, 4), 4)

    def rows_of(hf):
        return pl.ds(HALVES[hf][0], HALVES[hf][1])

    def far_copy(m, hf, dev):
        k = hf * 4 + lax.rem(m, 4)
        return remote(
            part.at[m, rows_of(hf)], far.at[k, pl.ds(0, HALVES[hf][1])], first_send.at[hf, m], far_recv.at[k], dev
        )

    def near_copy(m, hf, side, sem, dev):
        k = lax.rem(m, 4)
        return remote(
            part.at[m, rows_of(hf)], near.at[side, k, rows_of(hf)], sem, near_recv.at[side, k, hf], dev
        )

    def first_sends(m):
        d = distance(m)

        @pl.when(d == 2)
        def _():
            far_copy(m, 0, y_dn).start()
            far_copy(m, 1, y_up).start()

        @pl.when(d == 1)
        def _():
            near_copy(m, 1, 1, first_send.at[1, m], y_dn).start()

        @pl.when(d == 3)
        def _():
            near_copy(m, 0, 0, first_send.at[0, m], y_up).start()

    def row_loop(hf):
        return pl.loop(0, HALVES[hf][1] // 16)

    def merge(m):
        d = distance(m)
        for hf in range(2):

            @pl.when(d == 1 + 2 * hf)
            def _():
                far_copy(m, hf, y_up if hf == 0 else y_dn).wait_recv()
                k = hf * 4 + lax.rem(m, 4)

                @row_loop(hf)
                def _(r):
                    rows = pl.ds(pl.multiple_of(HALVES[hf][0] + r * 16, 16), 16)
                    theirs = far[k, pl.ds(pl.multiple_of(r * 16, 16), 16), :]
                    part[m, rows, :] = (part[m, rows, :].astype(F32) + theirs.astype(F32)).astype(BF)

                near_copy(m, hf, 1 - hf, merge_send.at[m], y_dn if hf == 0 else y_up).start()

    def is_mine(m):
        return lax.rem(lax.div(m, 2), 2) == xl

    def cross_copy(m, hf):
        k = lax.rem(m, 2)
        return remote(
            part.at[m, rows_of(hf)], cross.at[k, rows_of(hf)], cross_send.at[k, hf], cross_recv.at[k, hf], x_near
        )

    def sum_up(m):
        @pl.when(distance(m) == 0)
        def _():
            k = lax.rem(m, 4)
            own = is_mine(m)
            for hf in range(2):
                near_copy(m, hf, 0, first_send.at[hf, m], y_dn).wait_recv()
                near_copy(m, hf, 1, first_send.at[hf, m], y_up).wait_recv()

                def total(r):
                    rows = pl.ds(pl.multiple_of(HALVES[hf][0] + r * 16, 16), 16)
                    sides = near[0, k, rows, :].astype(F32) + near[1, k, rows, :].astype(F32)
                    return rows, part[m, rows, :].astype(F32) + sides

                @pl.when(own)
                def _():
                    @row_loop(hf)
                    def _(r):
                        rows, value = total(r)
                        mine[lax.rem(m, 2), rows, :] = value

                @pl.when(jnp.logical_not(own))
                def _():
                    @row_loop(hf)
                    def _(r):
                        rows, value = total(r)
                        part[m, rows, :] = value.astype(BF)

                    cross_copy(m, hf).start()

    def finish(m):
        @pl.when(jnp.logical_and(distance(m) == 0, is_mine(m)))
        def _():
            k = lax.rem(m, 2)
            for hf in range(2):
                cross_copy(m, hf).wait_recv()

                @row_loop(hf)
                def _(r):
                    rows = pl.ds(pl.multiple_of(HALVES[hf][0] + r * 16, 16), 16)
                    here = pl.ds(pl.multiple_of(k * UT + HALVES[hf][0] + r * 16, 16), 16)
                    grad = mine[k, rows, :] + cross[k, rows, :].astype(F32)
                    gu_out[here, :] = (grad * f_up[here, :]).astype(BF)
                    gg_out[here, :] = (grad * f_gate[here, :]).astype(BF)

    @pl.loop(0, N1 + N2 + 1)
    def _(i):
        before = jnp.maximum(i - 1, 0)

        @pl.loop(table(before, MERGED), table(i, MERGED))
        def _(k):
            merge(unit(k))

        @pl.loop(table(before, SUMMED), table(i, SUMMED))
        def _(k):
            sum_up(unit(k))

        @pl.loop(table(before, FINISHED), table(i, FINISHED))
        def _(k):
            finish(unit(k))

        @pl.when(i < N1)
        def _():
            k0 = 2 * i - 1 + jnp.where(i < 2, 1, 0) - jnp.where(i == 8, 1, 0)
            both = jnp.logical_and(i != 1, i != 7)
            m0 = unit(k0)
            m1 = jnp.where(both, unit(k0 + 1), m0)
            for j in range(2):
                sib_copy(m0, j, 1 - core).wait_recv()

            @pl.when(both)
            def _():
                for j in range(2):
                    sib_copy(m1, j, 1 - core).wait_recv()

            lhs = jnp.concatenate(
                [panel[pl.ds(2 * m0, 2)].reshape(UT, D), panel[pl.ds(2 * m1, 2)].reshape(UT, D)], axis=0
            )
            res = lax.dot_general(lhs, wt[...], (((1,), (0,)), ((), ())), preferred_element_type=F32).astype(BF)
            part[m0] = res[:UT]
            first_sends(m0)

            @pl.when(both)
            def _():
                part[m1] = res[UT:]
                first_sends(m1)

        @pl.when(i == N1)
        def _():
            hid_copy(c_opp, hup_send.at[1], y_dn).wait_recv()
            hid_copy(p_own, hx_send.at[0], x_near).wait_recv()
            hid_copy(p_prev, hx_send.at[2], x_near).wait_recv()
            hid_copy(p_opp, hdn_send.at[1], y_up).wait_recv()

        @pl.when(jnp.logical_and(i >= N1, i < N1 + N2))
        def _():
            t = i - N1
            cols = pl.ds(pl.multiple_of(t * DT, DT), DT)
            res = lax.dot_general(
                hid[...].reshape(8 * OT, H),
                panel[:, :, cols].reshape(8 * OT, DT),
                (((0,), (0,)), ((), ())),
                preferred_element_type=F32,
            )
            gd_out[:, cols] = res.astype(BF)

        @pl.when(i == HID_NEAR)
        def _():
            hid_copy(c_next, hup_send.at[0], y_up).wait_recv()
            hid_copy(c_next, hx_send.at[1], x_near).start()
            hid_copy(c_prev, hdn_send.at[0], y_dn).wait_recv()
            hid_copy(c_prev, hup_send.at[1], y_up).start()
            hid_copy(c_prev, hx_send.at[2], x_near).start()

        @pl.when(i == HID_FAR)
        def _():
            hid_copy(p_next, hx_send.at[1], x_near).wait_recv()
            hid_copy(p_next, hdn_send.at[1], y_dn).start()

        @pl.when(jnp.logical_and(i >= 1, i < 6))
        def _():
            pass_on(lax.div(i + 2, 2), jnp.where(lax.rem(i, 2) == 0, xh, 1 - xh))

        @pl.when(i == 7)
        def _():
            z_opp = wrap(z + 4, 8)
            for j in range(2):
                go_up(z_opp, j).wait_recv()
                to_sib(z_opp, j).start()
                go_dn(8 + z_opp, j).wait_recv()
                to_sib(8 + z_opp, j).start()

    for j in range(2):
        to_far(j).wait_send()

    @pl.loop(0, 4)
    def _(d):
        for xh_ in range(2):
            below = xh_ * 8 + wrap(z - d, 8)
            above = xh_ * 8 + wrap(z + d, 8)

            @pl.when(jnp.logical_or(d < 3, xh_ == 0))
            def _():
                for j in range(2):
                    go_up(below, j).wait_send()

            @pl.when(jnp.logical_or(d < 3, xh_ == 1))
            def _():
                for j in range(2):
                    go_dn(above, j).wait_send()

    @pl.loop(0, 16)
    def _(m):
        for j in range(2):
            to_sib(m, j).wait_send()
        d = distance(m)

        @pl.when(d >= 2)
        def _():
            far_copy(m, 0, y_dn).wait_send()

        @pl.when(jnp.logical_or(d == 1, d == 2))
        def _():
            far_copy(m, 1, y_up).wait_send()

        for hf in range(2):

            @pl.when(d == 1 + 2 * hf)
            def _():
                near_copy(m, hf, 1 - hf, merge_send.at[m], y_dn if hf == 0 else y_up).wait_send()

    for k in range(2):
        hid_copy(col, hup_send.at[k], y_up).wait_send()
        hid_copy(col, hdn_send.at[k], y_dn).wait_send()
    for k in range(3):
        hid_copy(col, hx_send.at[k], x_near).wait_send()
    for k in range(2):
        for hf in range(2):
            cross_copy(k, hf).wait_send()


W_PARTS = 4


def write_out(gd, gg, gu, gd_out, gg_out, gu_out, gd_sem, sem):
    n = H // W_PARTS
    copies = [
        pltpu.make_async_copy(gd.at[pl.ds(k * n, n)], gd_out.at[pl.ds(k * n, n)], gd_sem.at[k])
        for k in range(W_PARTS)
    ]
    copies += [
        pltpu.make_async_copy(gg, gg_out, sem.at[0]),
        pltpu.make_async_copy(gu, gu_out, sem.at[1]),
    ]
    for c in copies:
        c.start()
    for c in copies:
        c.wait()


def on_device(out_grad, gate_pre, up_pre, w_down):
    dma = pltpu.SemaphoreType.DMA
    any_space = pl.BlockSpec(memory_space=pl.ANY)
    results = pl.pallas_call(
        kernel,
        out_shape=(
            pltpu.VMEM((H, D), BF),
            pltpu.VMEM((OT, H), BF),
            pltpu.VMEM((OT, H), BF),
        ),
        in_specs=[any_space] * 4,
        out_specs=(pl.BlockSpec(memory_space=pltpu.VMEM),) * 3,
        scratch_shapes=[
            pltpu.VMEM((32, TB, D), BF),
            pltpu.VMEM((H, D), BF),
            pltpu.VMEM((D, H), BF),
            pltpu.VMEM((16, UT, H), BF),
            pltpu.VMEM((8, OT, H), BF),
            pltpu.VMEM((8, HALVES[0][1], H), BF),
            pltpu.VMEM((2, 4, UT, H), BF),
            pltpu.VMEM((2, UT, H), BF),
            pltpu.VMEM((2, UT, H), F32),
            pltpu.VMEM((OT, H), BF),
            pltpu.VMEM((OT, H), BF),
            pltpu.VMEM((OT, H), F32),
            pltpu.VMEM((OT, H), F32),
            dma((4,)),
            dma((2, 16)), dma((2, 16)), dma((2, 16)), dma((2, 16)), dma((2, 16)), dma((2,)),
            dma((8,)), dma((2,)), dma((2,)), dma((3,)),
            dma((8,)), dma((2, 4, 2)), dma((2, 16)), dma((16,)), dma((2, 2)), dma((2, 2)),
        ],
        compiler_params=pltpu.CompilerParams(
            collective_id=0, has_side_effects=True, vmem_limit_bytes=56 * 2**20
        ),
        cost_estimate=pl.CostEstimate(flops=4 * 1792 * H * D, bytes_accessed=9 * 2**20, transcendentals=OT * H),
        name="swiglu_down_backward",
    )(out_grad, gate_pre, up_pre, w_down)
    results = [pltpu.with_memory_space_constraint(r, pltpu.VMEM) for r in results]
    return pl.pallas_call(
        write_out,
        out_shape=tuple(jax.ShapeDtypeStruct(r.shape, r.dtype) for r in results),
        in_specs=[any_space] * 3,
        out_specs=(any_space,) * 3,
        scratch_shapes=[dma((W_PARTS,)), dma((2,))],
        compiler_params=pltpu.CompilerParams(vmem_limit_bytes=2**20),
        name="write_out",
    )(*results)


def solution(mesh):
    return jax.shard_map(
        on_device,
        mesh=mesh,
        in_specs=(P("row", "col"), P("col", "row"), P("col", "row"), P("row", "col")),
        out_specs=(P("row", "col"), P("col", "row"), P("col", "row")),
        check_vma=False,
    )
```

```python
import jax
import jax.numpy as jnp
from jax import lax
from jax.experimental import pallas as pl
from jax.experimental.pallas import tpu as pltpu
from jax.sharding import PartitionSpec as P

MESH = pl.DeviceIdType.MESH
BF = jnp.bfloat16
F32 = jnp.float32

TB = 56
UT = 112
HALVES = ((0, 64), (64, 48))
H = 896
D = 2048
DH = D // 2
OT = 224
N1 = 9
N2 = 4
DT = D // N2


def wrap(a, n):
    return lax.rem(a + n, n)


def table(i, values):
    total = jnp.int32(0)
    for k, v in enumerate(values):
        if v != 0:
            total = total + jnp.where(i == k, v, 0)
    return total


MERGED = [0, 0, 2, 3, 5, 7, 9, 11, 11, 14, 16, 16, 16, 16]
SUMMED = [0, 0, 0, 0, 2, 3, 5, 7, 7, 11, 14, 16, 16, 16]
FINISHED = [0, 0, 0, 0, 0, 0, 2, 3, 3, 7, 11, 14, 14, 16]
HID_NEAR = 2
HID_FAR = 4


def kernel(
    og, gate, up, w_hbm, gd_out, gg_out, gu_out,
    panel, w, wt, part, hid, far, near, cross, mine, gate_v, up_v, f_up, f_gate,
    in_sem, ring_recv, sib_recv, up_send, dn_send, sib_send, xh_send,
    hid_recv, hup_send, hdn_send, hx_send,
    far_recv, near_recv, first_send, merge_send, cross_recv, cross_send,
):
    row = lax.axis_index("row")
    col = lax.axis_index("col")
    xh = lax.div(row, 16)
    z = lax.rem(lax.div(row, 2), 8)
    core = lax.rem(row, 2)
    y = lax.div(col, 2)
    xl = lax.rem(col, 2)

    def at(xh_, z_, core_, y_, xl_):
        return ((xh_ * 8 + z_) * 2 + core_, y_ * 2 + xl_)

    y_next, y_prev, y_opp = wrap(y + 1, 4), wrap(y - 1, 4), wrap(y + 2, 4)
    z_up = at(xh, wrap(z + 1, 8), core, y, xl)
    z_dn = at(xh, wrap(z - 1, 8), core, y, xl)
    x_far = at(1 - xh, z, core, y, xl)
    sib = at(xh, z, 1 - core, y, xl)
    y_up = at(xh, z, core, y_next, xl)
    y_dn = at(xh, z, core, y_prev, xl)
    x_near = at(xh, z, core, y, 1 - xl)

    def remote(src, dst, ssem, rsem, dev):
        return pltpu.make_async_remote_copy(
            src_ref=src, dst_ref=dst, send_sem=ssem, recv_sem=rsem, device_id=dev, device_id_type=MESH
        )

    load_gate = pltpu.make_async_copy(gate, gate_v, in_sem.at[0])
    load_up = pltpu.make_async_copy(up, up_v, in_sem.at[1])
    load_w = pltpu.make_async_copy(w_hbm, w, in_sem.at[2])
    own_unit = xh * 8 + z
    far_unit = (1 - xh) * 8 + z
    load_og = pltpu.make_async_copy(og, panel.at[own_unit * 2 + core], in_sem.at[3])

    barrier = pltpu.get_barrier_semaphore()
    for dev in (z_up, z_dn, x_far, sib, y_up, y_dn, x_near):
        pl.semaphore_signal(barrier, inc=1, device_id=dev, device_id_type=MESH)
    load_gate.start()
    load_up.start()
    load_og.start()
    load_w.start()
    load_gate.wait()
    load_up.wait()

    @pl.loop(0, OT // 16)
    def _(k):
        rows = pl.ds(pl.multiple_of(k * 16, 16), 16)
        g = gate_v[rows, :].astype(F32)
        u = up_v[rows, :].astype(F32)
        s = 1.0 / (1.0 + jnp.exp(-g))
        silu = g * s
        hid[col, rows, :] = (silu * u).astype(BF)
        f_up[rows, :] = silu
        f_gate[rows, :] = u * s * (1.0 + g * (1.0 - s))

    pl.semaphore_wait(barrier, 7)

    def half(j):
        return pl.ds(j * DH, DH)

    def ring_copy(unit, j, ssem, dev, own=False):
        block = panel.at[unit * 2 + core, :, half(j)]
        return remote(og.at[:, half(j)] if own else block, block, ssem, ring_recv.at[j, unit], dev)

    def go_up(unit, j, own=False):
        return ring_copy(unit, j, up_send.at[j, unit], z_up, own)

    def go_dn(unit, j, own=False):
        return ring_copy(unit, j, dn_send.at[j, unit], z_dn, own)

    def to_far(j):
        return ring_copy(own_unit, j, xh_send.at[j], x_far, True)

    def sib_copy(unit, j, core_, own=False):
        block = panel.at[unit * 2 + core_, :, half(j)]
        return remote(
            og.at[:, half(j)] if own else block, block, sib_send.at[j, unit], sib_recv.at[j, unit], sib
        )

    def to_sib(unit, j, own=False):
        return sib_copy(unit, j, core, own)

    for j in range(2):
        to_far(j).start()
        go_up(own_unit, j, True).start()
        go_dn(own_unit, j, True).start()
    for j in range(2):
        to_sib(own_unit, j, True).start()

    def hid_copy(c, ssem, dev):
        return remote(hid.at[c], hid.at[c], ssem, hid_recv.at[c], dev)

    c_next, c_prev, c_opp = y_next * 2 + xl, y_prev * 2 + xl, y_opp * 2 + xl
    p_own, p_next, p_prev, p_opp = (y_ * 2 + 1 - xl for y_ in (y, y_next, y_prev, y_opp))
    hid_copy(col, hup_send.at[0], y_up).start()
    hid_copy(col, hdn_send.at[0], y_dn).start()

    def pass_on(d, xh_):
        from_dn = xh_ * 8 + wrap(z - d, 8)
        from_up = xh_ * 8 + wrap(z + d, 8)
        for j in range(2):
            go_up(from_dn, j).wait_recv()

            @pl.when(jnp.logical_or(d < 3, xh_ == 0))
            def _():
                go_up(from_dn, j).start()

            to_sib(from_dn, j).start()
            go_dn(from_up, j).wait_recv()

            @pl.when(jnp.logical_or(d < 3, xh_ == 1))
            def _():
                go_dn(from_up, j).start()

            to_sib(from_up, j).start()

    load_w.wait()

    @pl.loop(0, 8)
    def _(k):
        cols = pl.ds(pl.multiple_of(k * 256, 256), 256)
        wt[cols, :] = w[:, cols].T

    for j in range(2):
        to_far_in = ring_copy(far_unit, j, xh_send.at[j], x_far)
        to_far_in.wait_recv()
        go_up(far_unit, j).start()
        go_dn(far_unit, j).start()
        to_sib(far_unit, j).start()
    hid_copy(col, hx_send.at[0], x_near).start()
    pass_on(1, xh)

    load_og.wait()

    def unit(k):
        d = lax.div(k + 2, 4)
        own = jnp.logical_or(k == 0, jnp.logical_and(lax.rem(k + 2, 4) < 2, k < 15))
        return jnp.where(own, xh, 1 - xh) * 8 + jnp.where(lax.rem(k, 2) == 0, wrap(z - d, 8), wrap(z + d, 8))

    def distance(m):
        return wrap(y - lax.div(m, 4), 4)

    def rows_of(hf):
        return pl.ds(HALVES[hf][0], HALVES[hf][1])

    def far_copy(m, hf, dev):
        k = hf * 4 + lax.rem(m, 4)
        return remote(
            part.at[m, rows_of(hf)], far.at[k, pl.ds(0, HALVES[hf][1])], first_send.at[hf, m], far_recv.at[k], dev
        )

    def near_copy(m, hf, side, sem, dev):
        k = lax.rem(m, 4)
        return remote(
            part.at[m, rows_of(hf)], near.at[side, k, rows_of(hf)], sem, near_recv.at[side, k, hf], dev
        )

    def first_sends(m):
        d = distance(m)

        @pl.when(d == 2)
        def _():
            far_copy(m, 0, y_dn).start()
            far_copy(m, 1, y_up).start()

        @pl.when(d == 1)
        def _():
            near_copy(m, 1, 1, first_send.at[1, m], y_dn).start()

        @pl.when(d == 3)
        def _():
            near_copy(m, 0, 0, first_send.at[0, m], y_up).start()

    def row_loop(hf):
        return pl.loop(0, HALVES[hf][1] // 16)

    def merge(m):
        d = distance(m)
        for hf in range(2):

            @pl.when(d == 1 + 2 * hf)
            def _():
                far_copy(m, hf, y_up if hf == 0 else y_dn).wait_recv()
                k = hf * 4 + lax.rem(m, 4)

                @row_loop(hf)
                def _(r):
                    rows = pl.ds(pl.multiple_of(HALVES[hf][0] + r * 16, 16), 16)
                    theirs = far[k, pl.ds(pl.multiple_of(r * 16, 16), 16), :]
                    part[m, rows, :] = (part[m, rows, :].astype(F32) + theirs.astype(F32)).astype(BF)

                near_copy(m, hf, 1 - hf, merge_send.at[m], y_dn if hf == 0 else y_up).start()

    def is_mine(m):
        return lax.rem(lax.div(m, 2), 2) == xl

    def cross_copy(m, hf):
        k = lax.rem(m, 2)
        return remote(
            part.at[m, rows_of(hf)], cross.at[k, rows_of(hf)], cross_send.at[k, hf], cross_recv.at[k, hf], x_near
        )

    def sum_up(m):
        @pl.when(distance(m) == 0)
        def _():
            k = lax.rem(m, 4)
            own = is_mine(m)
            for hf in range(2):
                near_copy(m, hf, 0, first_send.at[hf, m], y_dn).wait_recv()
                near_copy(m, hf, 1, first_send.at[hf, m], y_up).wait_recv()

                def total(r):
                    rows = pl.ds(pl.multiple_of(HALVES[hf][0] + r * 16, 16), 16)
                    sides = near[0, k, rows, :].astype(F32) + near[1, k, rows, :].astype(F32)
                    return rows, part[m, rows, :].astype(F32) + sides

                @pl.when(own)
                def _():
                    @row_loop(hf)
                    def _(r):
                        rows, value = total(r)
                        mine[lax.rem(m, 2), rows, :] = value

                @pl.when(jnp.logical_not(own))
                def _():
                    @row_loop(hf)
                    def _(r):
                        rows, value = total(r)
                        part[m, rows, :] = value.astype(BF)

                    cross_copy(m, hf).start()

    def finish(m):
        @pl.when(jnp.logical_and(distance(m) == 0, is_mine(m)))
        def _():
            k = lax.rem(m, 2)
            for hf in range(2):
                cross_copy(m, hf).wait_recv()

                @row_loop(hf)
                def _(r):
                    rows = pl.ds(pl.multiple_of(HALVES[hf][0] + r * 16, 16), 16)
                    here = pl.ds(pl.multiple_of(k * UT + HALVES[hf][0] + r * 16, 16), 16)
                    grad = mine[k, rows, :] + cross[k, rows, :].astype(F32)
                    gu_out[here, :] = (grad * f_up[here, :]).astype(BF)
                    gg_out[here, :] = (grad * f_gate[here, :]).astype(BF)

    @pl.loop(0, N1 + N2 + 1)
    def _(i):
        before = jnp.maximum(i - 1, 0)

        @pl.loop(table(before, MERGED), table(i, MERGED))
        def _(k):
            merge(unit(k))

        @pl.loop(table(before, SUMMED), table(i, SUMMED))
        def _(k):
            sum_up(unit(k))

        @pl.loop(table(before, FINISHED), table(i, FINISHED))
        def _(k):
            finish(unit(k))

        @pl.when(i < N1)
        def _():
            k0 = 2 * i - 1 + jnp.where(i < 2, 1, 0) - jnp.where(i == 8, 1, 0)
            both = jnp.logical_and(i != 1, i != 7)
            m0 = unit(k0)
            m1 = jnp.where(both, unit(k0 + 1), m0)
            for j in range(2):
                sib_copy(m0, j, 1 - core).wait_recv()

            @pl.when(both)
            def _():
                for j in range(2):
                    sib_copy(m1, j, 1 - core).wait_recv()

            lhs = jnp.concatenate(
                [panel[pl.ds(2 * m0, 2)].reshape(UT, D), panel[pl.ds(2 * m1, 2)].reshape(UT, D)], axis=0
            )
            res = lax.dot_general(lhs, wt[...], (((1,), (0,)), ((), ())), preferred_element_type=F32).astype(BF)
            part[m0] = res[:UT]
            first_sends(m0)

            @pl.when(both)
            def _():
                part[m1] = res[UT:]
                first_sends(m1)

        @pl.when(i == N1)
        def _():
            hid_copy(c_opp, hup_send.at[1], y_dn).wait_recv()
            hid_copy(p_own, hx_send.at[0], x_near).wait_recv()
            hid_copy(p_prev, hx_send.at[2], x_near).wait_recv()
            hid_copy(p_opp, hdn_send.at[1], y_up).wait_recv()

        @pl.when(jnp.logical_and(i >= N1, i < N1 + N2))
        def _():
            t = i - N1
            cols = pl.ds(pl.multiple_of(t * DT, DT), DT)
            res = lax.dot_general(
                hid[...].reshape(8 * OT, H),
                panel[:, :, cols].reshape(8 * OT, DT),
                (((0,), (0,)), ((), ())),
                preferred_element_type=F32,
            )
            gd_out[:, cols] = res.astype(BF)

        @pl.when(i == HID_NEAR)
        def _():
            hid_copy(c_next, hup_send.at[0], y_up).wait_recv()
            hid_copy(c_next, hx_send.at[1], x_near).start()
            hid_copy(c_prev, hdn_send.at[0], y_dn).wait_recv()
            hid_copy(c_prev, hup_send.at[1], y_up).start()
            hid_copy(c_prev, hx_send.at[2], x_near).start()

        @pl.when(i == HID_FAR)
        def _():
            hid_copy(p_next, hx_send.at[1], x_near).wait_recv()
            hid_copy(p_next, hdn_send.at[1], y_dn).start()

        @pl.when(jnp.logical_and(i >= 1, i < 6))
        def _():
            pass_on(lax.div(i + 2, 2), jnp.where(lax.rem(i, 2) == 0, xh, 1 - xh))

        @pl.when(i == 7)
        def _():
            z_opp = wrap(z + 4, 8)
            for j in range(2):
                go_up(z_opp, j).wait_recv()
                to_sib(z_opp, j).start()
                go_dn(8 + z_opp, j).wait_recv()
                to_sib(8 + z_opp, j).start()

    for j in range(2):
        to_far(j).wait_send()

    @pl.loop(0, 4)
    def _(d):
        for xh_ in range(2):
            below = xh_ * 8 + wrap(z - d, 8)
            above = xh_ * 8 + wrap(z + d, 8)

            @pl.when(jnp.logical_or(d < 3, xh_ == 0))
            def _():
                for j in range(2):
                    go_up(below, j).wait_send()

            @pl.when(jnp.logical_or(d < 3, xh_ == 1))
            def _():
                for j in range(2):
                    go_dn(above, j).wait_send()

    @pl.loop(0, 16)
    def _(m):
        for j in range(2):
            to_sib(m, j).wait_send()
        d = distance(m)

        @pl.when(d >= 2)
        def _():
            far_copy(m, 0, y_dn).wait_send()

        @pl.when(jnp.logical_or(d == 1, d == 2))
        def _():
            far_copy(m, 1, y_up).wait_send()

        for hf in range(2):

            @pl.when(d == 1 + 2 * hf)
            def _():
                near_copy(m, hf, 1 - hf, merge_send.at[m], y_dn if hf == 0 else y_up).wait_send()

    for k in range(2):
        hid_copy(col, hup_send.at[k], y_up).wait_send()
        hid_copy(col, hdn_send.at[k], y_dn).wait_send()
    for k in range(3):
        hid_copy(col, hx_send.at[k], x_near).wait_send()
    for k in range(2):
        for hf in range(2):
            cross_copy(k, hf).wait_send()


W_PARTS = 4


def write_out(gd, gg, gu, gd_out, gg_out, gu_out, gd_sem, sem):
    n = H // W_PARTS
    copies = [
        pltpu.make_async_copy(gd.at[pl.ds(k * n, n)], gd_out.at[pl.ds(k * n, n)], gd_sem.at[k])
        for k in range(W_PARTS)
    ]
    copies += [
        pltpu.make_async_copy(gg, gg_out, sem.at[0]),
        pltpu.make_async_copy(gu, gu_out, sem.at[1]),
    ]
    for c in copies:
        c.start()
    for c in copies:
        c.wait()


def on_device(out_grad, gate_pre, up_pre, w_down):
    dma = pltpu.SemaphoreType.DMA
    any_space = pl.BlockSpec(memory_space=pl.ANY)
    results = pl.pallas_call(
        kernel,
        out_shape=(
            pltpu.VMEM((H, D), BF),
            pltpu.VMEM((OT, H), BF),
            pltpu.VMEM((OT, H), BF),
        ),
        in_specs=[any_space] * 4,
        out_specs=(pl.BlockSpec(memory_space=pltpu.VMEM),) * 3,
        scratch_shapes=[
            pltpu.VMEM((32, TB, D), BF),
            pltpu.VMEM((H, D), BF),
            pltpu.VMEM((D, H), BF),
            pltpu.VMEM((16, UT, H), BF),
            pltpu.VMEM((8, OT, H), BF),
            pltpu.VMEM((8, HALVES[0][1], H), BF),
            pltpu.VMEM((2, 4, UT, H), BF),
            pltpu.VMEM((2, UT, H), BF),
            pltpu.VMEM((2, UT, H), F32),
            pltpu.VMEM((OT, H), BF),
            pltpu.VMEM((OT, H), BF),
            pltpu.VMEM((OT, H), F32),
            pltpu.VMEM((OT, H), F32),
            dma((4,)),
            dma((2, 16)), dma((2, 16)), dma((2, 16)), dma((2, 16)), dma((2, 16)), dma((2,)),
            dma((8,)), dma((2,)), dma((2,)), dma((3,)),
            dma((8,)), dma((2, 4, 2)), dma((2, 16)), dma((16,)), dma((2, 2)), dma((2, 2)),
        ],
        compiler_params=pltpu.CompilerParams(
            collective_id=0, has_side_effects=True, vmem_limit_bytes=56 * 2**20
        ),
        cost_estimate=pl.CostEstimate(flops=4 * 1792 * H * D, bytes_accessed=9 * 2**20, transcendentals=OT * H),
        name="swiglu_down_backward",
    )(out_grad, gate_pre, up_pre, w_down)
    results = [pltpu.with_memory_space_constraint(r, pltpu.VMEM) for r in results]
    return pl.pallas_call(
        write_out,
        out_shape=tuple(jax.ShapeDtypeStruct(r.shape, r.dtype) for r in results),
        in_specs=[any_space] * 3,
        out_specs=(any_space,) * 3,
        scratch_shapes=[dma((W_PARTS,)), dma((2,))],
        compiler_params=pltpu.CompilerParams(vmem_limit_bytes=2**20),
        name="write_out",
    )(*results)


def solution(mesh):
    return jax.shard_map(
        on_device,
        mesh=mesh,
        in_specs=(P("row", "col"), P("col", "row"), P("col", "row"), P("row", "col")),
        out_specs=(P("row", "col"), P("col", "row"), P("col", "row")),
        check_vma=False,
    )
```

```python
import jax
import jax.numpy as jnp
from jax import lax
from jax.experimental import pallas as pl
from jax.experimental.pallas import tpu as pltpu
from jax.sharding import PartitionSpec as P

MESH = pl.DeviceIdType.MESH
BF = jnp.bfloat16
F32 = jnp.float32

TB = 56
UT = 112
HALVES = ((0, 64), (64, 48))
H = 896
D = 2048
DH = D // 2
OT = 224
N1 = 9
N2 = 4
DT = D // N2


def wrap(a, n):
    return lax.rem(a + n, n)


def table(i, values):
    total = jnp.int32(0)
    for k, v in enumerate(values):
        if v != 0:
            total = total + jnp.where(i == k, v, 0)
    return total


MERGED = [0, 0, 2, 3, 5, 7, 9, 9, 9, 14, 16, 16, 16, 16]
SUMMED = [0, 0, 0, 0, 2, 3, 5, 5, 5, 9, 14, 16, 16, 16]
FINISHED = [0, 0, 0, 0, 0, 0, 2, 2, 2, 5, 9, 14, 14, 16]
HID_NEAR = 2
HID_FAR = 4


def kernel(
    og, gate, up, w_hbm, gd_out, gg_out, gu_out,
    panel, w, wt, part, hid, far, near, cross, mine, gate_v, up_v, f_up, f_gate,
    in_sem, ring_recv, sib_recv, up_send, dn_send, sib_send, xh_send,
    hid_recv, hup_send, hdn_send, hx_send,
    far_recv, near_recv, first_send, merge_send, cross_recv, cross_send,
):
    row = lax.axis_index("row")
    col = lax.axis_index("col")
    xh = lax.div(row, 16)
    z = lax.rem(lax.div(row, 2), 8)
    core = lax.rem(row, 2)
    y = lax.div(col, 2)
    xl = lax.rem(col, 2)

    def at(xh_, z_, core_, y_, xl_):
        return ((xh_ * 8 + z_) * 2 + core_, y_ * 2 + xl_)

    y_next, y_prev, y_opp = wrap(y + 1, 4), wrap(y - 1, 4), wrap(y + 2, 4)
    z_up = at(xh, wrap(z + 1, 8), core, y, xl)
    z_dn = at(xh, wrap(z - 1, 8), core, y, xl)
    x_far = at(1 - xh, z, core, y, xl)
    sib = at(xh, z, 1 - core, y, xl)
    y_up = at(xh, z, core, y_next, xl)
    y_dn = at(xh, z, core, y_prev, xl)
    x_near = at(xh, z, core, y, 1 - xl)

    def remote(src, dst, ssem, rsem, dev):
        return pltpu.make_async_remote_copy(
            src_ref=src, dst_ref=dst, send_sem=ssem, recv_sem=rsem, device_id=dev, device_id_type=MESH
        )

    load_gate = pltpu.make_async_copy(gate, gate_v, in_sem.at[0])
    load_up = pltpu.make_async_copy(up, up_v, in_sem.at[1])
    load_w = pltpu.make_async_copy(w_hbm, w, in_sem.at[2])
    own_unit = xh * 8 + z
    far_unit = (1 - xh) * 8 + z
    load_og = pltpu.make_async_copy(og, panel.at[own_unit * 2 + core], in_sem.at[3])

    barrier = pltpu.get_barrier_semaphore()
    for dev in (z_up, z_dn, x_far, sib, y_up, y_dn, x_near):
        pl.semaphore_signal(barrier, inc=1, device_id=dev, device_id_type=MESH)
    load_gate.start()
    load_up.start()
    load_og.start()
    load_w.start()
    load_gate.wait()
    load_up.wait()

    @pl.loop(0, OT // 16)
    def _(k):
        rows = pl.ds(pl.multiple_of(k * 16, 16), 16)
        g = gate_v[rows, :].astype(F32)
        u = up_v[rows, :].astype(F32)
        s = 1.0 / (1.0 + jnp.exp(-g))
        silu = g * s
        hid[col, rows, :] = (silu * u).astype(BF)
        f_up[rows, :] = silu
        f_gate[rows, :] = u * s * (1.0 + g * (1.0 - s))

    pl.semaphore_wait(barrier, 7)

    def half(j):
        return pl.ds(j * DH, DH)

    def ring_copy(unit, j, ssem, dev, own=False):
        block = panel.at[unit * 2 + core, :, half(j)]
        return remote(og.at[:, half(j)] if own else block, block, ssem, ring_recv.at[j, unit], dev)

    def go_up(unit, j, own=False):
        return ring_copy(unit, j, up_send.at[j, unit], z_up, own)

    def go_dn(unit, j, own=False):
        return ring_copy(unit, j, dn_send.at[j, unit], z_dn, own)

    def to_far(j):
        return ring_copy(own_unit, j, xh_send.at[j], x_far, True)

    def sib_copy(unit, j, core_, own=False):
        block = panel.at[unit * 2 + core_, :, half(j)]
        return remote(
            og.at[:, half(j)] if own else block, block, sib_send.at[j, unit], sib_recv.at[j, unit], sib
        )

    def to_sib(unit, j, own=False):
        return sib_copy(unit, j, core, own)

    for j in range(2):
        to_far(j).start()
        go_up(own_unit, j, True).start()
        go_dn(own_unit, j, True).start()
    for j in range(2):
        to_sib(own_unit, j, True).start()

    def hid_copy(c, ssem, dev):
        return remote(hid.at[c], hid.at[c], ssem, hid_recv.at[c], dev)

    c_next, c_prev, c_opp = y_next * 2 + xl, y_prev * 2 + xl, y_opp * 2 + xl
    p_own, p_next, p_prev, p_opp = (y_ * 2 + 1 - xl for y_ in (y, y_next, y_prev, y_opp))
    hid_copy(col, hup_send.at[0], y_up).start()
    hid_copy(col, hdn_send.at[0], y_dn).start()

    def pass_on(d, xh_):
        from_dn = xh_ * 8 + wrap(z - d, 8)
        from_up = xh_ * 8 + wrap(z + d, 8)
        for j in range(2):
            go_up(from_dn, j).wait_recv()

            @pl.when(jnp.logical_or(d < 3, xh_ == 0))
            def _():
                go_up(from_dn, j).start()

            to_sib(from_dn, j).start()
            go_dn(from_up, j).wait_recv()

            @pl.when(jnp.logical_or(d < 3, xh_ == 1))
            def _():
                go_dn(from_up, j).start()

            to_sib(from_up, j).start()

    load_w.wait()

    @pl.loop(0, 8)
    def _(k):
        cols = pl.ds(pl.multiple_of(k * 256, 256), 256)
        wt[cols, :] = w[:, cols].T

    for j in range(2):
        to_far_in = ring_copy(far_unit, j, xh_send.at[j], x_far)
        to_far_in.wait_recv()
        go_up(far_unit, j).start()
        go_dn(far_unit, j).start()
        to_sib(far_unit, j).start()
    hid_copy(col, hx_send.at[0], x_near).start()
    pass_on(1, xh)

    load_og.wait()

    def unit(k):
        d = lax.div(k + 2, 4)
        own = jnp.logical_or(k == 0, jnp.logical_and(lax.rem(k + 2, 4) < 2, k < 15))
        return jnp.where(own, xh, 1 - xh) * 8 + jnp.where(lax.rem(k, 2) == 0, wrap(z - d, 8), wrap(z + d, 8))

    def distance(m):
        return wrap(y - lax.div(m, 4), 4)

    def rows_of(hf):
        return pl.ds(HALVES[hf][0], HALVES[hf][1])

    def far_copy(m, hf, dev):
        k = hf * 4 + lax.rem(m, 4)
        return remote(
            part.at[m, rows_of(hf)], far.at[k, pl.ds(0, HALVES[hf][1])], first_send.at[hf, m], far_recv.at[k], dev
        )

    def near_copy(m, hf, side, sem, dev):
        k = lax.rem(m, 4)
        return remote(
            part.at[m, rows_of(hf)], near.at[side, k, rows_of(hf)], sem, near_recv.at[side, k, hf], dev
        )

    def first_sends(m):
        d = distance(m)

        @pl.when(d == 2)
        def _():
            far_copy(m, 0, y_dn).start()
            far_copy(m, 1, y_up).start()

        @pl.when(d == 1)
        def _():
            near_copy(m, 1, 1, first_send.at[1, m], y_dn).start()

        @pl.when(d == 3)
        def _():
            near_copy(m, 0, 0, first_send.at[0, m], y_up).start()

    def row_loop(hf):
        return pl.loop(0, HALVES[hf][1] // 16)

    def merge(m):
        d = distance(m)
        for hf in range(2):

            @pl.when(d == 1 + 2 * hf)
            def _():
                far_copy(m, hf, y_up if hf == 0 else y_dn).wait_recv()
                k = hf * 4 + lax.rem(m, 4)

                @row_loop(hf)
                def _(r):
                    rows = pl.ds(pl.multiple_of(HALVES[hf][0] + r * 16, 16), 16)
                    theirs = far[k, pl.ds(pl.multiple_of(r * 16, 16), 16), :]
                    part[m, rows, :] = (part[m, rows, :].astype(F32) + theirs.astype(F32)).astype(BF)

                near_copy(m, hf, 1 - hf, merge_send.at[m], y_dn if hf == 0 else y_up).start()

    def is_mine(m):
        return lax.rem(lax.div(m, 2), 2) == xl

    def cross_copy(m, hf):
        k = lax.rem(m, 2)
        return remote(
            part.at[m, rows_of(hf)], cross.at[k, rows_of(hf)], cross_send.at[k, hf], cross_recv.at[k, hf], x_near
        )

    def sum_up(m):
        @pl.when(distance(m) == 0)
        def _():
            k = lax.rem(m, 4)
            own = is_mine(m)
            for hf in range(2):
                near_copy(m, hf, 0, first_send.at[hf, m], y_dn).wait_recv()
                near_copy(m, hf, 1, first_send.at[hf, m], y_up).wait_recv()

                def total(r):
                    rows = pl.ds(pl.multiple_of(HALVES[hf][0] + r * 16, 16), 16)
                    sides = near[0, k, rows, :].astype(F32) + near[1, k, rows, :].astype(F32)
                    return rows, part[m, rows, :].astype(F32) + sides

                @pl.when(own)
                def _():
                    @row_loop(hf)
                    def _(r):
                        rows, value = total(r)
                        mine[lax.rem(m, 2), rows, :] = value

                @pl.when(jnp.logical_not(own))
                def _():
                    @row_loop(hf)
                    def _(r):
                        rows, value = total(r)
                        part[m, rows, :] = value.astype(BF)

                    cross_copy(m, hf).start()

    def finish(m):
        @pl.when(jnp.logical_and(distance(m) == 0, is_mine(m)))
        def _():
            k = lax.rem(m, 2)
            for hf in range(2):
                cross_copy(m, hf).wait_recv()

                @row_loop(hf)
                def _(r):
                    rows = pl.ds(pl.multiple_of(HALVES[hf][0] + r * 16, 16), 16)
                    here = pl.ds(pl.multiple_of(k * UT + HALVES[hf][0] + r * 16, 16), 16)
                    grad = mine[k, rows, :] + cross[k, rows, :].astype(F32)
                    gu_out[here, :] = (grad * f_up[here, :]).astype(BF)
                    gg_out[here, :] = (grad * f_gate[here, :]).astype(BF)

    @pl.loop(0, N1 + N2 + 1)
    def _(i):
        before = jnp.maximum(i - 1, 0)

        @pl.loop(table(before, MERGED), table(i, MERGED))
        def _(k):
            merge(unit(k))

        @pl.loop(table(before, SUMMED), table(i, SUMMED))
        def _(k):
            sum_up(unit(k))

        @pl.loop(table(before, FINISHED), table(i, FINISHED))
        def _(k):
            finish(unit(k))

        @pl.when(i < N1)
        def _():
            k0 = 2 * i - 1 + jnp.where(i < 2, 1, 0) - jnp.where(i == 8, 1, 0)
            both = jnp.logical_and(i != 1, i != 7)
            m0 = unit(k0)
            m1 = jnp.where(both, unit(k0 + 1), m0)
            for j in range(2):
                sib_copy(m0, j, 1 - core).wait_recv()

            @pl.when(both)
            def _():
                for j in range(2):
                    sib_copy(m1, j, 1 - core).wait_recv()

            lhs = jnp.concatenate(
                [panel[pl.ds(2 * m0, 2)].reshape(UT, D), panel[pl.ds(2 * m1, 2)].reshape(UT, D)], axis=0
            )
            res = lax.dot_general(lhs, wt[...], (((1,), (0,)), ((), ())), preferred_element_type=F32).astype(BF)
            part[m0] = res[:UT]
            first_sends(m0)

            @pl.when(both)
            def _():
                part[m1] = res[UT:]
                first_sends(m1)

        @pl.when(i == N1)
        def _():
            hid_copy(c_opp, hup_send.at[1], y_dn).wait_recv()
            hid_copy(p_own, hx_send.at[0], x_near).wait_recv()
            hid_copy(p_prev, hx_send.at[2], x_near).wait_recv()
            hid_copy(p_opp, hdn_send.at[1], y_up).wait_recv()

        @pl.when(jnp.logical_and(i >= N1, i < N1 + N2))
        def _():
            t = i - N1
            cols = pl.ds(pl.multiple_of(t * DT, DT), DT)
            res = lax.dot_general(
                hid[...].reshape(8 * OT, H),
                panel[:, :, cols].reshape(8 * OT, DT),
                (((0,), (0,)), ((), ())),
                preferred_element_type=F32,
            )
            gd_out[:, cols] = res.astype(BF)

        @pl.when(i == HID_NEAR)
        def _():
            hid_copy(c_next, hup_send.at[0], y_up).wait_recv()
            hid_copy(c_next, hx_send.at[1], x_near).start()
            hid_copy(c_prev, hdn_send.at[0], y_dn).wait_recv()
            hid_copy(c_prev, hup_send.at[1], y_up).start()
            hid_copy(c_prev, hx_send.at[2], x_near).start()

        @pl.when(i == HID_FAR)
        def _():
            hid_copy(p_next, hx_send.at[1], x_near).wait_recv()
            hid_copy(p_next, hdn_send.at[1], y_dn).start()

        @pl.when(jnp.logical_and(i >= 1, i < 6))
        def _():
            pass_on(lax.div(i + 2, 2), jnp.where(lax.rem(i, 2) == 0, xh, 1 - xh))

        @pl.when(i == 7)
        def _():
            z_opp = wrap(z + 4, 8)
            for j in range(2):
                go_up(z_opp, j).wait_recv()
                to_sib(z_opp, j).start()
                go_dn(8 + z_opp, j).wait_recv()
                to_sib(8 + z_opp, j).start()

    for j in range(2):
        to_far(j).wait_send()

    @pl.loop(0, 4)
    def _(d):
        for xh_ in range(2):
            below = xh_ * 8 + wrap(z - d, 8)
            above = xh_ * 8 + wrap(z + d, 8)

            @pl.when(jnp.logical_or(d < 3, xh_ == 0))
            def _():
                for j in range(2):
                    go_up(below, j).wait_send()

            @pl.when(jnp.logical_or(d < 3, xh_ == 1))
            def _():
                for j in range(2):
                    go_dn(above, j).wait_send()

    @pl.loop(0, 16)
    def _(m):
        for j in range(2):
            to_sib(m, j).wait_send()
        d = distance(m)

        @pl.when(d >= 2)
        def _():
            far_copy(m, 0, y_dn).wait_send()

        @pl.when(jnp.logical_or(d == 1, d == 2))
        def _():
            far_copy(m, 1, y_up).wait_send()

        for hf in range(2):

            @pl.when(d == 1 + 2 * hf)
            def _():
                near_copy(m, hf, 1 - hf, merge_send.at[m], y_dn if hf == 0 else y_up).wait_send()

    for k in range(2):
        hid_copy(col, hup_send.at[k], y_up).wait_send()
        hid_copy(col, hdn_send.at[k], y_dn).wait_send()
    for k in range(3):
        hid_copy(col, hx_send.at[k], x_near).wait_send()
    for k in range(2):
        for hf in range(2):
            cross_copy(k, hf).wait_send()


W_PARTS = 4


def write_out(gd, gg, gu, gd_out, gg_out, gu_out, gd_sem, sem):
    n = H // W_PARTS
    copies = [
        pltpu.make_async_copy(gd.at[pl.ds(k * n, n)], gd_out.at[pl.ds(k * n, n)], gd_sem.at[k])
        for k in range(W_PARTS)
    ]
    copies += [
        pltpu.make_async_copy(gg, gg_out, sem.at[0]),
        pltpu.make_async_copy(gu, gu_out, sem.at[1]),
    ]
    for c in copies:
        c.start()
    for c in copies:
        c.wait()


def on_device(out_grad, gate_pre, up_pre, w_down):
    dma = pltpu.SemaphoreType.DMA
    any_space = pl.BlockSpec(memory_space=pl.ANY)
    results = pl.pallas_call(
        kernel,
        out_shape=(
            pltpu.VMEM((H, D), BF),
            pltpu.VMEM((OT, H), BF),
            pltpu.VMEM((OT, H), BF),
        ),
        in_specs=[any_space] * 4,
        out_specs=(pl.BlockSpec(memory_space=pltpu.VMEM),) * 3,
        scratch_shapes=[
            pltpu.VMEM((32, TB, D), BF),
            pltpu.VMEM((H, D), BF),
            pltpu.VMEM((D, H), BF),
            pltpu.VMEM((16, UT, H), BF),
            pltpu.VMEM((8, OT, H), BF),
            pltpu.VMEM((8, HALVES[0][1], H), BF),
            pltpu.VMEM((2, 4, UT, H), BF),
            pltpu.VMEM((2, UT, H), BF),
            pltpu.VMEM((2, UT, H), F32),
            pltpu.VMEM((OT, H), BF),
            pltpu.VMEM((OT, H), BF),
            pltpu.VMEM((OT, H), F32),
            pltpu.VMEM((OT, H), F32),
            dma((4,)),
            dma((2, 16)), dma((2, 16)), dma((2, 16)), dma((2, 16)), dma((2, 16)), dma((2,)),
            dma((8,)), dma((2,)), dma((2,)), dma((3,)),
            dma((8,)), dma((2, 4, 2)), dma((2, 16)), dma((16,)), dma((2, 2)), dma((2, 2)),
        ],
        compiler_params=pltpu.CompilerParams(
            collective_id=0, has_side_effects=True, vmem_limit_bytes=56 * 2**20
        ),
        cost_estimate=pl.CostEstimate(flops=4 * 1792 * H * D, bytes_accessed=9 * 2**20, transcendentals=OT * H),
        name="swiglu_down_backward",
    )(out_grad, gate_pre, up_pre, w_down)
    results = [pltpu.with_memory_space_constraint(r, pltpu.VMEM) for r in results]
    return pl.pallas_call(
        write_out,
        out_shape=tuple(jax.ShapeDtypeStruct(r.shape, r.dtype) for r in results),
        in_specs=[any_space] * 3,
        out_specs=(any_space,) * 3,
        scratch_shapes=[dma((W_PARTS,)), dma((2,))],
        compiler_params=pltpu.CompilerParams(vmem_limit_bytes=2**20),
        name="write_out",
    )(*results)


def solution(mesh):
    return jax.shard_map(
        on_device,
        mesh=mesh,
        in_specs=(P("row", "col"), P("col", "row"), P("col", "row"), P("row", "col")),
        out_specs=(P("row", "col"), P("col", "row"), P("col", "row")),
        check_vma=False,
    )
```
